256 devices in a mesh: ctx: 64 (over x, z, core), tp: 4 (over y).
Axes of the slice: x: 4, y: 4, z: 8, core: 2. Of those that a mesh axis runs over, the one named last changes fastest.
Arguments:
- queries: bfloat16 [32768, 8192], P('ctx', 'tp')
- keys: bfloat16 [32768, 1024], P('ctx', 'tp')
- values: bfloat16 [32768, 1024], P('ctx', 'tp'), may hold values from -6 to 6
- block_lengths: int32 [64], replicated, may hold values from 256 to 512, as said below
- decode_query_rows: bfloat16 [64, 8192], P('ctx', 'tp')
- out_weight: bfloat16 [8192, 8192], P('tp', 'ctx'), may hold values from -0.0625 to 0.0625
Outputs:
- block_out: bfloat16 [32768, 8192], P('ctx', 'tp')
- decode_out: bfloat16 [64, 8192], P(None, 'ctx')
The draws below stay inside these ranges and needn't reach their ends.
Inputs may be any that keep to these rules, and one draw needn't show every extreme that they name: `block_lengths`: each block has between 256 and 512 live slots, at its lowest offsets; in every draw some block is full.
All inputs are finite; a program needn't handle non-finite values.
Results may differ from the reference program's by a relative error of at most 0.0056.
Values may be sent and summed in bfloat16 or wider, within the bound.
No kernel may reach another device: no remote copies, remote signals or barrier semaphores. Data moves between devices by JAX's collectives and lax.ppermute only.
A program may use at most 192 MiB of HBM per device.

```python
import jax
import jax.numpy as jnp
from jax import lax

D = 8192
QUERY_HEADS = 64
KEY_VALUE_HEADS = 8
HEAD_SIZE = 128
BLOCK_SLOTS = 512
CONTEXT_SLOTS = 32768
DECODE_ROWS = 64


def shared_keys(key):
    return jax.random.normal(key, (CONTEXT_SLOTS, KEY_VALUE_HEADS * HEAD_SIZE), jnp.float32)


def draw_keys(key, part):
    key_base = shared_keys(key)
    return jnp.clip(key_base, -6.0, 6.0).astype(jnp.bfloat16)


def draw_queries(key, part):
    key = jax.random.fold_in(key, 2)
    key_noise = jax.random.fold_in(key, 0)
    noise_part = jnp.clip(jax.random.normal(key_noise, (CONTEXT_SLOTS, QUERY_HEADS * HEAD_SIZE), jnp.float32), -6.0, 6.0)
    return noise_part.astype(jnp.bfloat16)


def draw_decode_query_rows(key, part):
    key = jax.random.fold_in(key, 3)
    key_noise = jax.random.fold_in(key, 0)
    noise_part = jnp.clip(jax.random.normal(key_noise, (DECODE_ROWS, QUERY_HEADS * HEAD_SIZE), jnp.float32), -6.0, 6.0)
    return noise_part.astype(jnp.bfloat16)


def draw_block_lengths(key, part):
    key = jax.random.fold_in(key, 4)
    key_len, key_full = jax.random.split(key)
    number_of_blocks = CONTEXT_SLOTS // BLOCK_SLOTS
    lengths = jax.random.randint(key_len, (number_of_blocks,), BLOCK_SLOTS // 2, BLOCK_SLOTS + 1)
    full_slot = jax.random.randint(key_full, (), 0, number_of_blocks)
    return jnp.where(jnp.arange(number_of_blocks) == full_slot, BLOCK_SLOTS, lengths).astype(jnp.int32)


def level_of(rng, shape, cuts, least, high):
    loudness, own = 1.0, jax.random.fold_in(rng, 6)
    for axis_at, blocks in cuts:
        steps = jnp.exp(jax.random.uniform(jax.random.fold_in(own, axis_at), (blocks,), jnp.float32, least / len(cuts), high / len(cuts)))
        loudness = loudness * jnp.repeat(steps, shape[axis_at] // blocks).reshape([-1 if axis == axis_at else 1 for axis in range(len(shape))])
    return loudness


def normal_values(rng, dims, width, most, cuts=(), kind=jnp.bfloat16):
    array = width * jax.random.normal(rng, dims, jnp.float32)
    if cuts:
        array = array * level_of(rng, dims, cuts, -0.22, 0.18)
    return jnp.clip(array, -most, most).astype(kind)


def setup_inputs(seed: int = 0) -> dict:
    streams_of = jax.random.split(jax.random.key(seed), 7)
    return {
        "queries": draw_queries(jax.random.fold_in(streams_of[6], 71), 0),
        "keys": draw_keys(jax.random.fold_in(streams_of[6], 71), 0),
        "values": normal_values(streams_of[2], (CONTEXT_SLOTS, KEY_VALUE_HEADS * HEAD_SIZE), 1.0, 6.0, ((0, 64), (1, 4))),
        "block_lengths": draw_block_lengths(jax.random.fold_in(streams_of[6], 71), 0),
        "decode_query_rows": draw_decode_query_rows(jax.random.fold_in(streams_of[6], 71), 0),
        "out_weight": normal_values(streams_of[5], (QUERY_HEADS * HEAD_SIZE, D), (QUERY_HEADS * HEAD_SIZE) ** -0.5, 0.0625, ((0, 4), (1, 64))),
    }


def reference(queries, keys, values, block_lengths, decode_query_rows, out_weight):
    number_of_blocks = CONTEXT_SLOTS // BLOCK_SLOTS
    group_width = QUERY_HEADS // KEY_VALUE_HEADS
    inv_root = HEAD_SIZE ** -0.5
    blocked_queries = queries.reshape(number_of_blocks, BLOCK_SLOTS, KEY_VALUE_HEADS, group_width, HEAD_SIZE)
    blocked_keys = keys.reshape(number_of_blocks, BLOCK_SLOTS, KEY_VALUE_HEADS, HEAD_SIZE)
    blocked_values = values.reshape(number_of_blocks, BLOCK_SLOTS, KEY_VALUE_HEADS, HEAD_SIZE)
    anchor_keys = blocked_keys[0].astype(jnp.float32)
    anchor_values = blocked_values[0].astype(jnp.float32)
    anchor_len = block_lengths[0]
    offsets = jnp.arange(BLOCK_SLOTS, dtype=jnp.int32)

    def one_block(items):
        query_part, key_part, value_part, own_len, block_index = items
        query_f = query_part.astype(jnp.float32)
        anchor_scores = jnp.einsum('ikgd,jkd->kgij', query_f, anchor_keys) * inv_root
        own_scores = jnp.einsum('ikgd,jkd->kgij', query_f, key_part.astype(jnp.float32)) * inv_root
        anchor_ok = (offsets < anchor_len) & (block_index > 0)
        own_ok = (offsets[None, :] <= offsets[:, None]) & (offsets[None, :] < own_len)
        scores = jnp.concatenate([jnp.where(anchor_ok, anchor_scores, -1e30), jnp.where(own_ok, own_scores, -1e30)], axis=-1)
        top_score = jnp.max(scores, axis=-1, keepdims=True)
        powers = jnp.exp(scores - top_score)
        totals = jnp.sum(powers, axis=-1)
        shares = powers.astype(jnp.bfloat16).astype(jnp.float32)
        value_cat = jnp.concatenate([anchor_values, value_part.astype(jnp.float32)], axis=0)
        weighted = jnp.einsum('kgij,jkd->ikgd', shares, value_cat)
        result = weighted / jnp.transpose(totals, (2, 0, 1))[..., None]
        result = jnp.where((offsets < own_len)[:, None, None, None], result, 0.0)
        return result.reshape(BLOCK_SLOTS, QUERY_HEADS * HEAD_SIZE).astype(jnp.bfloat16)

    block_out = lax.map(one_block, (blocked_queries, blocked_keys, blocked_values, block_lengths, jnp.arange(number_of_blocks, dtype=jnp.int32)))
    block_out = block_out.reshape(CONTEXT_SLOTS, QUERY_HEADS * HEAD_SIZE)

    decode_float_rows = decode_query_rows.reshape(DECODE_ROWS, KEY_VALUE_HEADS, group_width, HEAD_SIZE).astype(jnp.float32)

    def decode_part(items):
        key_part, value_part, own_len = items
        scores = jnp.einsum('rkgd,jkd->kgrj', decode_float_rows, key_part.astype(jnp.float32)) * inv_root
        scores = jnp.where(offsets < own_len, scores, -1e30)
        top_score = jnp.max(scores, axis=-1)
        powers = jnp.exp(scores - top_score[..., None])
        totals = jnp.sum(powers, axis=-1)
        shares = powers.astype(jnp.bfloat16).astype(jnp.float32)
        weighted = jnp.einsum('kgrj,jkd->kgrd', shares, value_part.astype(jnp.float32))
        return top_score, totals, weighted

    maxima, totals, weighted = lax.map(decode_part, (blocked_keys, blocked_values, block_lengths))
    overall = jnp.max(maxima, axis=0)
    factors = jnp.exp(maxima - overall)
    total_sum = jnp.sum(totals * factors, axis=0)
    weighted_sum = jnp.sum(weighted * factors[..., None], axis=0)
    attn = jnp.transpose(weighted_sum / total_sum[..., None], (2, 0, 1, 3)).reshape(DECODE_ROWS, QUERY_HEADS * HEAD_SIZE).astype(jnp.bfloat16)
    decode_out = jnp.dot(attn, out_weight, preferred_element_type=jnp.float32).astype(jnp.bfloat16)
    return block_out, decode_out
```

```python
import functools
import math

import jax
import jax.numpy as jnp
from jax import lax
from jax.experimental import pallas as pl
from jax.experimental.pallas import tpu as pltpu
from jax.sharding import PartitionSpec as P

HEAD = 128
GROUP = 8
KV = 2
SLOTS = 512
HALF = 256
ROWS = 64
NX, NZ, NCORE, NTP = 4, 8, 2, 4
WIDE = KV * GROUP * HEAD
MESSAGE = WIDE + 128
EXP2_SCALE = HEAD**-0.5 * math.log2(math.e)
NEG = -1e30
NT = (((1,), (1,)), ((), ()))


def ctx_at(x, z, core):
    return (x * NZ + z) * NCORE + core


XC_GROUPS = [[ctx_at(x, z, c) for x in range(NX) for c in range(NCORE)] for z in range(NZ)]
Z_GROUPS = [[ctx_at(x, z, c) for z in range(NZ)] for x in range(NX) for c in range(NCORE)]


def qk(q, k):
    return lax.dot_general(q, k, NT, preferred_element_type=jnp.float32)


def pv(p, v):
    return jnp.dot(p.astype(jnp.bfloat16), v, preferred_element_type=jnp.float32)


def block_kernel(info, q_ref, k_ref, v_ref, one_ref, two_ref, *rest):
    o_ref = rest[-1]
    own_len, anchor_len, core = info[0], info[1], info[2]
    one, two = one_ref[...], two_ref[...]
    ka = jnp.where(core == 0, one, two)
    va = jnp.where(core == 0, two, one)
    lane = lax.broadcasted_iota(jnp.int32, (HALF, HALF), 1)
    row = lax.broadcasted_iota(jnp.int32, (HALF, HALF), 0)
    for part in range(2):
        rows = pl.ds(part * HALF, HALF)
        q = q_ref[rows, :]
        own = qk(q, k_ref[: HALF * (part + 1), :])
        anchor = qk(q, ka)
        pieces = [
            jnp.where(lane < anchor_len, anchor[:, :HALF], NEG),
            jnp.where(lane + HALF < anchor_len, anchor[:, HALF:], NEG),
        ]
        if part:
            pieces.append(own[:, :HALF])
        pieces.append(jnp.where(lane <= row, own[:, part * HALF :], NEG))
        scores = jnp.concatenate(pieces, axis=1)
        top = jnp.max(scores, axis=1, keepdims=True)
        powers = jnp.exp2((scores - top) * EXP2_SCALE)
        total = jnp.sum(powers, axis=1, keepdims=True)
        weighted = pv(powers[:, :SLOTS], va) + pv(powers[:, SLOTS:], v_ref[: HALF * (part + 1), :])
        live = lax.broadcasted_iota(jnp.int32, (HALF, HEAD), 0) + part * HALF < own_len
        o_ref[rows, :] = jnp.where(live, weighted / total, 0.0).astype(o_ref.dtype)


def block_pass(kv, info, queries, keys, values, one, two, out):
    head = lambda g, info: (0, kv * GROUP + g)
    shared = lambda g, info: (0, kv)
    specs = [pl.BlockSpec((SLOTS, HEAD), head)] + [pl.BlockSpec((SLOTS, HEAD), shared)] * 4
    operands = [queries, keys, values, one, two]
    aliases = {}
    if out is not None:
        specs.append(pl.BlockSpec(memory_space=pl.ANY))
        operands.append(out)
        aliases = {6: 0}
    return pl.pallas_call(
        block_kernel,
        grid_spec=pltpu.PrefetchScalarGridSpec(
            num_scalar_prefetch=1,
            grid=(GROUP,),
            in_specs=specs,
            out_specs=pl.BlockSpec((SLOTS, HEAD), head),
        ),
        out_shape=jax.ShapeDtypeStruct(queries.shape, jnp.bfloat16),
        input_output_aliases=aliases,
        compiler_params=pltpu.CompilerParams(vmem_limit_bytes=32 << 20),
        cost_estimate=pl.CostEstimate(
            flops=GROUP * SLOTS * SLOTS * HEAD * 8, bytes_accessed=4 << 20, transcendentals=GROUP * SLOTS * 1024
        ),
        name="block_pass",
    )(info, *operands)


def pack_lse(lse):
    lane = lax.broadcasted_iota(jnp.int32, lse.shape, 1)
    high = lse.astype(jnp.bfloat16).astype(jnp.float32)
    rest = lse - high
    mid = rest.astype(jnp.bfloat16).astype(jnp.float32)
    low = rest - mid
    return jnp.where(lane < 16, high, jnp.where(lane < 32, mid, jnp.where(lane < 48, low, 0.0))).astype(jnp.bfloat16)


def decode_kernel(info, q_ref, k_ref, v_ref, o_ref):
    own_len = info[0]
    lane = lax.broadcasted_iota(jnp.int32, (GROUP * ROWS, SLOTS), 1)
    spot = lax.broadcasted_iota(jnp.int32, (ROWS, 128), 1) % 16
    lse = jnp.zeros((ROWS, 128), jnp.float32)
    for kv in range(KV):
        cols = pl.ds(kv * HEAD, HEAD)
        q = jnp.concatenate(
            [q_ref[:, pl.ds((kv * GROUP + g) * HEAD, HEAD)] for g in range(GROUP)], axis=0
        )
        scores = jnp.where(lane < own_len, qk(q, k_ref[:, cols]), NEG)
        top = jnp.max(scores, axis=1, keepdims=True)
        powers = jnp.exp2((scores - top) * EXP2_SCALE)
        total = jnp.sum(powers, axis=1, keepdims=True)
        weighted = pv(powers, v_ref[:, cols]) / total
        level = top * EXP2_SCALE + jnp.log2(total)
        for g in range(GROUP):
            rows = slice(g * ROWS, (g + 1) * ROWS)
            head = kv * GROUP + g
            o_ref[:, pl.ds(head * HEAD, HEAD)] = weighted[rows].astype(jnp.bfloat16)
            lse = jnp.where(spot == head, level[rows], lse)
    o_ref[:, pl.ds(WIDE, 128)] = pack_lse(lse)


def decode(info, rows, keys, values):
    return pl.pallas_call(
        decode_kernel,
        in_specs=[pl.BlockSpec(memory_space=pltpu.SMEM)] + [pl.BlockSpec(memory_space=pltpu.VMEM)] * 3,
        out_specs=pl.BlockSpec(memory_space=pltpu.VMEM),
        out_shape=jax.ShapeDtypeStruct((ROWS, MESSAGE), jnp.bfloat16),
        compiler_params=pltpu.CompilerParams(vmem_limit_bytes=32 << 20),
        cost_estimate=pl.CostEstimate(
            flops=4 * KV * GROUP * ROWS * SLOTS * HEAD, bytes_accessed=1 << 20, transcendentals=KV * GROUP * ROWS * SLOTS
        ),
        name="decode_part",
    )(info, rows, keys, values)


def merge_kernel(last, in_ref, o_ref):
    sources, rows, _ = in_ref.shape
    levels = []
    for s in range(sources):
        parts = in_ref[s, :, pl.ds(WIDE, 128)].astype(jnp.float32)
        levels.append(parts + pltpu.roll(parts, 112, 1) + pltpu.roll(parts, 96, 1))
    top = functools.reduce(jnp.maximum, levels)
    shares = [jnp.exp2(level - top) for level in levels]
    total = functools.reduce(jnp.add, shares)
    shares = [share / total for share in shares]
    copies = o_ref.shape[0]
    for head in range(KV * GROUP):
        cols = pl.ds(head * HEAD, HEAD)
        merged = jnp.zeros((rows, HEAD), jnp.float32)
        for s in range(sources):
            merged += shares[s][:, head : head + 1] * in_ref[s, :, cols].astype(jnp.float32)
        merged = merged.astype(jnp.bfloat16)
        for copy in range(copies):
            o_ref[copy, :, cols] = merged
    if not last:
        lane = lax.broadcasted_iota(jnp.int32, (rows, 128), 1)
        level = jnp.where(lane < 16, top + jnp.log2(total), 0.0)
        level = level + pltpu.roll(level, 16, 1) + pltpu.roll(level, 32, 1)
        packed = pack_lse(level)
        for copy in range(copies):
            o_ref[copy, :, pl.ds(WIDE, 128)] = packed


def merge(parts, copies, last):
    _, rows, _ = parts.shape
    return pl.pallas_call(
        functools.partial(merge_kernel, last),
        in_specs=[pl.BlockSpec(memory_space=pltpu.VMEM)],
        out_specs=pl.BlockSpec(memory_space=pltpu.VMEM),
        out_shape=jax.ShapeDtypeStruct((copies, rows, WIDE if last else MESSAGE), jnp.bfloat16),
        cost_estimate=pl.CostEstimate(flops=1 << 20, bytes_accessed=1 << 19, transcendentals=1 << 12),
        name="merge_parts",
    )(parts)


def fetch_anchor(keys, values, at):
    x, z, core = at
    perm = lambda block, pairs: lax.ppermute(block, "ctx", pairs)
    with jax.named_scope("anchor_core"):
        sent = perm(values, [(ctx_at(0, 0, 0), ctx_at(0, 0, 1))])
        held = jnp.where(core == 0, keys, sent)

    def across_x(core, zs):
        return [[(ctx_at(0, q, core), ctx_at(t, q, core)) for q in zs] for t in (1, 3, 2)]

    def across_z(core, xs, hops):
        return [[(ctx_at(q, s, core), ctx_at(q, t, core)) for q in xs for s, t in hop] for hop in hops]

    far = [[(0, 3)], [(0, 5)]]
    near = [[(0, 1), (3, 2), (5, 6)], [(0, 7), (3, 4)]]
    zs, xs = range(NZ), range(NX)
    stages = [
        (across_x(0, [0]), across_z(1, [0], far)),
        (across_z(0, xs, far), across_z(1, [0], near)),
        (across_z(0, xs, near), across_x(1, zs)),
    ]
    ctx = lax.axis_index("ctx")
    for number, (first, second) in enumerate(stages):
        with jax.named_scope(f"anchor_step{number}"):
            count = max(len(first), len(second))
            moves = [
                (first[i] if i < len(first) else []) + (second[i] if i < len(second) else []) for i in range(count)
            ]
            arrived = [perm(held, pairs) for pairs in moves]
            for block, pairs in zip(arrived, moves):
                hit = functools.reduce(jnp.logical_or, [ctx == target for _, target in pairs])
                held = jnp.where(hit, block, held)
    with jax.named_scope("anchor_swap"):
        other = perm(held, [(i, i ^ 1) for i in range(NX * NZ * NCORE)])
    return held, other


def body(queries, keys, values, block_lengths, decode_query_rows, out_weight):
    ctx = lax.axis_index("ctx")
    at = (ctx // (NZ * NCORE), (ctx // NCORE) % NZ, ctx % NCORE)
    own_len = block_lengths[ctx]
    anchor_len = jnp.where(ctx > 0, block_lengths[0], 0)
    info = jnp.stack([own_len, anchor_len, at[2]]).astype(jnp.int32)

    with jax.named_scope("rows_out"):
        spread = jnp.broadcast_to(decode_query_rows, (ROWS, WIDE))
        rows = lax.all_to_all(spread, "ctx", 0, 0, tiled=True)
    one, two = fetch_anchor(keys, values, at)

    message = decode(info, rows, keys, values)
    with jax.named_scope("parts_xc"):
        parts = lax.all_to_all(message, "ctx", 0, 0, axis_index_groups=XC_GROUPS, tiled=True)
    merged = merge(parts.reshape(8, 8, MESSAGE), NZ, False)
    with jax.named_scope("parts_z"):
        parts = lax.all_to_all(merged, "ctx", 0, 0, axis_index_groups=Z_GROUPS, tiled=True)
    attn = merge(parts, NX * NCORE, True)
    with jax.named_scope("attn_xc"):
        attn = lax.all_to_all(attn, "ctx", 0, 0, axis_index_groups=XC_GROUPS, tiled=True)
    projected = jnp.dot(attn.reshape(ROWS, WIDE), out_weight, preferred_element_type=jnp.float32)
    with jax.named_scope("tp_sum"):
        got = [lax.ppermute(projected, "tp", [(i, i ^ k) for i in range(NTP)]) for k in (1, 2, 3)]
        decode_out = ((projected + got[0]) + (got[1] + got[2])).astype(jnp.bfloat16)

    block_out = block_pass(0, info, queries, keys, values, one, two, None)
    block_out = block_pass(1, info, queries, keys, values, one, two, block_out)
    return block_out, decode_out


def solution(mesh):
    return jax.shard_map(
        body,
        mesh=mesh,
        in_specs=(
            P("ctx", "tp"),
            P("ctx", "tp"),
            P("ctx", "tp"),
            P(),
            P("ctx", "tp"),
            P("tp", "ctx"),
        ),
        out_specs=(P("ctx", "tp"), P(None, "ctx")),
        check_vma=False,
    )
```

```python
import functools
import math

import jax
import jax.numpy as jnp
from jax import lax
from jax.experimental import pallas as pl
from jax.experimental.pallas import tpu as pltpu
from jax.sharding import PartitionSpec as P

HEAD = 128
GROUP = 8
KV = 2
SLOTS = 512
HALF = 256
ROWS = 64
NX, NZ, NCORE, NTP = 4, 8, 2, 4
WIDE = KV * GROUP * HEAD
MESSAGE = WIDE + 128
EXP2_SCALE = HEAD**-0.5 * math.log2(math.e)
NEG = -1e30
NT = (((1,), (1,)), ((), ()))


def ctx_at(x, z, core):
    return (x * NZ + z) * NCORE + core


NEAR, FAR = 16, 4
NEAR_GROUPS = [
    [ctx_at(x, 2 * far + z, c) for x in range(NX) for z in range(2) for c in range(NCORE)] for far in range(FAR)
]
FAR_GROUPS = [
    [ctx_at(x, 2 * far + z, c) for far in range(FAR)] for x in range(NX) for z in range(2) for c in range(NCORE)
]
EACH = ROWS // NEAR


def qk(q, k):
    return lax.dot_general(q, k, NT, preferred_element_type=jnp.float32)


def pv(p, v):
    return jnp.dot(p.astype(jnp.bfloat16), v, preferred_element_type=jnp.float32)


def scaled(keys):
    wide = keys.astype(jnp.float32) * EXP2_SCALE
    high = wide.astype(jnp.bfloat16)
    return jnp.concatenate([high, (wide - high.astype(jnp.float32)).astype(jnp.bfloat16)], axis=1)


def with_ones(values):
    return jnp.concatenate([values, jnp.ones_like(values)], axis=1)


def max_of(pieces):
    tiles = [piece[:, i : i + HEAD] for piece in pieces for i in range(0, piece.shape[1], HEAD)]
    return jnp.max(functools.reduce(jnp.maximum, tiles), axis=1, keepdims=True)


def block_kernel(heads, lens, q_ref, k_ref, v_ref, one_ref, two_ref, *rest):
    o_ref = rest[-1]
    ctx = lax.axis_index("ctx")
    own_len, anchor_len = lens[ctx], lens[0]
    row = lax.broadcasted_iota(jnp.int32, (HALF, HALF), 0)
    lane = lax.broadcasted_iota(jnp.int32, (HALF, HALF), 1)

    def run(anchored):
        own_keys, own_values = scaled(k_ref[...]), with_ones(v_ref[...])
        if anchored:
            swap = lax.rem(ctx, NCORE) > 0
            one, two = one_ref[...], two_ref[...]
            anchor_keys = scaled(jnp.where(swap, two, one))
            anchor_values = with_ones(jnp.where(swap, one, two))

        def score(h, part):
            q = q_ref[pl.ds(part * HALF, HALF), h * HEAD : (h + 1) * HEAD]
            q = jnp.concatenate([q, q], axis=1)
            return qk(q, own_keys[: HALF * (part + 1)]), qk(q, anchor_keys) if anchored else None

        def share(part, own, anchor):
            pieces = [own[:, :HALF]] if part else []
            pieces.append(jnp.where(lane <= row, own[:, part * HALF :], NEG))
            if anchored:
                pieces += [anchor[:, :HALF], jnp.where(lane + HALF < anchor_len, anchor[:, HALF:], NEG)]
            top = max_of(pieces)
            shares = [jnp.exp2(piece - top).astype(jnp.bfloat16) for piece in pieces]
            cut = part + 1
            return jnp.concatenate(shares[:cut], axis=1), jnp.concatenate(shares[cut:], axis=1) if anchored else None

        def finish(h, part, own, anchor):
            both = jnp.dot(own, own_values[: HALF * (part + 1)], preferred_element_type=jnp.float32)
            if anchored:
                both += jnp.dot(anchor, anchor_values, preferred_element_type=jnp.float32)
            live = lax.broadcasted_iota(jnp.int32, (HALF, HEAD), 0) + part * HALF < own_len
            out = jnp.where(live, both[:, :HEAD] * (1.0 / both[:, HEAD:]), 0.0)
            o_ref[pl.ds(part * HALF, HALF), h * HEAD : (h + 1) * HEAD] = out.astype(o_ref.dtype)

        items = [(h, part) for h in range(heads) for part in range(2)]
        scores, shares = score(*items[0]), None
        for i, (h, part) in enumerate(items):
            later = score(*items[i + 1]) if i + 1 < len(items) else None
            now = share(part, *scores)
            if shares is not None:
                finish(*items[i - 1], *shares)
            scores, shares = later, now
        finish(*items[-1], *shares)

    pl.when(ctx > 0)(lambda: run(True))
    pl.when(ctx == 0)(lambda: run(False))


def block_pass(first, count, step, lens, queries, keys, values, one, two, out):
    head = lambda g, lens: (0, first // step + g)
    shared = lambda g, lens: (0, (first + g * step) // GROUP)
    specs = [pl.BlockSpec((SLOTS, step * HEAD), head)] + [pl.BlockSpec((SLOTS, HEAD), shared)] * 4
    operands = [queries, keys, values, one, two]
    aliases = {}
    if out is not None:
        specs.append(pl.BlockSpec(memory_space=pl.ANY))
        operands.append(out)
        aliases = {6: 0}
    return pl.pallas_call(
        functools.partial(block_kernel, step),
        grid_spec=pltpu.PrefetchScalarGridSpec(
            num_scalar_prefetch=1,
            grid=(count // step,),
            in_specs=specs,
            out_specs=pl.BlockSpec((SLOTS, step * HEAD), head),
        ),
        out_shape=jax.ShapeDtypeStruct(queries.shape, jnp.bfloat16),
        input_output_aliases=aliases,
        compiler_params=pltpu.CompilerParams(vmem_limit_bytes=56 << 20),
        cost_estimate=pl.CostEstimate(
            flops=count * SLOTS * SLOTS * HEAD * 8, bytes_accessed=4 << 20, transcendentals=count * SLOTS * 1024
        ),
        name="block_pass",
    )(lens, *operands)


def pack_lse(lse):
    lane = lax.broadcasted_iota(jnp.int32, lse.shape, 1)
    high = lse.astype(jnp.bfloat16).astype(jnp.float32)
    rest = lse - high
    mid = rest.astype(jnp.bfloat16).astype(jnp.float32)
    low = rest - mid
    return jnp.where(lane < 16, high, jnp.where(lane < 32, mid, jnp.where(lane < 48, low, 0.0))).astype(jnp.bfloat16)


def spread_kernel(row_ref, o_ref):
    row = row_ref[...].astype(jnp.float32)
    heads = jnp.concatenate([row[:, h * HEAD : (h + 1) * HEAD] for h in range(KV * GROUP)], axis=0)
    o_ref[...] = jnp.broadcast_to(heads.astype(jnp.bfloat16)[None], o_ref.shape)


def spread(row):
    return pl.pallas_call(
        spread_kernel,
        in_specs=[pl.BlockSpec(memory_space=pltpu.VMEM)],
        out_specs=pl.BlockSpec(memory_space=pltpu.VMEM),
        out_shape=jax.ShapeDtypeStruct((ROWS, KV * GROUP, HEAD), jnp.bfloat16),
        compiler_params=pltpu.CompilerParams(vmem_limit_bytes=8 << 20),
        cost_estimate=pl.CostEstimate(flops=1 << 16, bytes_accessed=1 << 18, transcendentals=0),
        name="spread_rows",
    )(row)


def decode_kernel(lens, q_ref, k_ref, v_ref, o_ref):
    own_len = lens[lax.axis_index("ctx")]
    lane = lax.broadcasted_iota(jnp.int32, (ROWS * GROUP, HALF), 1)
    spot = lax.broadcasted_iota(jnp.int32, (ROWS, 128), 1) % 16
    lse = jnp.zeros((ROWS, 128), jnp.float32)

    def put(cols, block):
        for n in range(NEAR):
            o_ref[n, :, cols] = block[n * EACH : (n + 1) * EACH]

    rows = q_ref[...].astype(jnp.float32)
    for kv in range(KV):
        cols = pl.ds(kv * HEAD, HEAD)
        q = rows[:, kv * GROUP : (kv + 1) * GROUP].reshape(ROWS * GROUP, HEAD).astype(jnp.bfloat16)
        scores = qk(q, k_ref[:, cols])
        near, far = scores[:, :HALF], jnp.where(lane + HALF < own_len, scores[:, HALF:], NEG)
        top = jnp.max(jnp.maximum(near, far), axis=1, keepdims=True)
        near, far = jnp.exp2((near - top) * EXP2_SCALE), jnp.exp2((far - top) * EXP2_SCALE)
        total = jnp.sum(near + far, axis=1, keepdims=True)
        weighted = pv(jnp.concatenate([near, far], axis=1), v_ref[:, cols]) * (1.0 / total)
        weighted = weighted.reshape(ROWS, GROUP, HEAD)
        level = jnp.broadcast_to(top * EXP2_SCALE + jnp.log2(total), (ROWS * GROUP, HEAD)).reshape(ROWS, GROUP, HEAD)
        for g in range(GROUP):
            head = kv * GROUP + g
            put(pl.ds(head * HEAD, HEAD), weighted[:, g].astype(jnp.bfloat16))
            lse = jnp.where(spot == head, level[:, g], lse)
    put(pl.ds(WIDE, 128), pack_lse(lse))


def decode(lens, rows, keys, values):
    return pl.pallas_call(
        decode_kernel,
        in_specs=[pl.BlockSpec(memory_space=pltpu.SMEM)] + [pl.BlockSpec(memory_space=pltpu.VMEM)] * 3,
        out_specs=pl.BlockSpec(memory_space=pltpu.VMEM),
        out_shape=jax.ShapeDtypeStruct((NEAR, EACH, MESSAGE), jnp.bfloat16),
        compiler_params=pltpu.CompilerParams(vmem_limit_bytes=32 << 20),
        cost_estimate=pl.CostEstimate(
            flops=4 * KV * GROUP * ROWS * SLOTS * HEAD, bytes_accessed=1 << 20, transcendentals=KV * GROUP * ROWS * SLOTS
        ),
        name="decode_part",
    )(lens, rows, keys, values)


def merge_kernel(last, in_ref, o_ref):
    tiles = in_ref.shape[0] // 2
    tile = lambda t, cols: jnp.concatenate([in_ref[2 * t + i, :, cols].astype(jnp.float32) for i in range(2)], axis=0)

    def across(op, parts):
        half = functools.reduce(op, parts)
        return op(half, pltpu.roll(half, EACH, 0))

    levels = []
    for t in range(tiles):
        parts = tile(t, pl.ds(WIDE, 128))
        levels.append(parts + pltpu.roll(parts, 112, 1) + pltpu.roll(parts, 96, 1))
    top = across(jnp.maximum, levels)
    shares = [jnp.exp2(level - top) for level in levels]
    total = across(jnp.add, shares)
    scale = 1.0 / total
    shares = [share * scale for share in shares]
    for head in range(KV * GROUP):
        cols = pl.ds(head * HEAD, HEAD)
        merged = across(jnp.add, [shares[t][:, head : head + 1] * tile(t, cols) for t in range(tiles)])
        o_ref[:, :, cols] = jnp.broadcast_to(merged[None, :EACH].astype(jnp.bfloat16), (o_ref.shape[0], EACH, HEAD))
    if not last:
        lane = lax.broadcasted_iota(jnp.int32, (2 * EACH, 128), 1)
        level = jnp.where(lane < 16, top + jnp.log2(total), 0.0)
        level = level + pltpu.roll(level, 16, 1) + pltpu.roll(level, 32, 1)
        o_ref[:, :, pl.ds(WIDE, 128)] = jnp.broadcast_to(pack_lse(level)[None, :EACH], (o_ref.shape[0], EACH, 128))


def merge(parts, copies, last):
    return pl.pallas_call(
        functools.partial(merge_kernel, last),
        in_specs=[pl.BlockSpec(memory_space=pltpu.VMEM)],
        out_specs=pl.BlockSpec(memory_space=pltpu.VMEM),
        out_shape=jax.ShapeDtypeStruct((copies, EACH, WIDE if last else MESSAGE), jnp.bfloat16),
        compiler_params=pltpu.CompilerParams(vmem_limit_bytes=8 << 20),
        cost_estimate=pl.CostEstimate(flops=1 << 20, bytes_accessed=1 << 19, transcendentals=1 << 12),
        name="merge_parts",
    )(parts)


def anchor_moves():
    near = [(0, 0), (1, 0), (0, 4), (1, 4)]
    keys_2 = [
        [((x, 0), (x + dx, dz)) for x in (0, 2)] for dx, dz in near[1:]
    ]
    values_2 = [
        [((0, z), (dx, z + dz)) for z in (0, 4)] for dx, dz in ((0, 2), (2, 0), (2, 2))
    ]
    keys_3 = [
        [((x, z), (x, (z + dz) % NZ)) for x in range(NX) for z in (0, 4)] for dz in (1, -1, 2)
    ]
    values_3 = [
        [((x, z), (x + dx, z + dz)) for x in (0, 2) for z in (0, 2, 4, 6)] for dx, dz in ((1, 0), (0, 1), (1, 1))
    ]

    def join(keys, values):
        return [
            [(ctx_at(*s, core), ctx_at(*t, core)) for core, pairs in enumerate(both) for s, t in pairs]
            for both in zip(keys, values)
        ]

    return join(keys_2, values_2), join(keys_3, values_3)


def fetch_anchor(keys, values, pins, later_pins):
    ctx = lax.axis_index("ctx")
    perm = lambda block, pairs: lax.ppermute(block, "ctx", pairs)

    def place(held, arrived, moves):
        for block, pairs in zip(arrived, moves):
            hit = functools.reduce(jnp.logical_or, [ctx == target for _, target in pairs])
            held = jnp.where(hit, block, held)
        return held

    with jax.named_scope("anchor_step1"):
        root = ctx_at(0, 0, 0)
        moves = [[(root, ctx_at(2, 0, 0))], [(root, ctx_at(0, 0, 1))], [(root, ctx_at(0, 4, 1))]]
        held = place(keys, [perm(block, pairs) for block, pairs in zip((keys, values, values), moves)], moves)
    for number, moves in enumerate(anchor_moves()):
        with jax.named_scope(f"anchor_step{number + 2}"):
            held, _ = lax.optimization_barrier((held, pins[number]))
            arrived = [perm(held, pairs) for pairs in moves]
            held, _ = lax.optimization_barrier((held, later_pins[number]))
            held = place(held, arrived, moves)
    with jax.named_scope("anchor_swap"):
        other = perm(held, [(i, i ^ 1) for i in range(NX * NZ * NCORE)])
    return held, other


def body(queries, keys, values, block_lengths, decode_query_rows, out_weight):
    with jax.named_scope("rows_out"):
        copies, keys, values = lax.optimization_barrier((spread(decode_query_rows), keys, values))
        rows = lax.all_to_all(copies, "ctx", 0, 0, tiled=True)
    message = decode(block_lengths, rows, keys, values)
    with jax.named_scope("parts_near"):
        parts = lax.all_to_all(message, "ctx", 0, 0, axis_index_groups=NEAR_GROUPS, tiled=True)
    merged = merge(parts, FAR, False)
    one, two = fetch_anchor(keys, values, (keys, message), (keys, keys))
    with jax.named_scope("parts_far"):
        parts = lax.all_to_all(merged, "ctx", 0, 0, axis_index_groups=FAR_GROUPS, tiled=True)
    attn = merge(parts, NEAR, True)
    with jax.named_scope("attn_near"):
        attn = lax.all_to_all(attn, "ctx", 0, 0, axis_index_groups=NEAR_GROUPS, tiled=True)
    projected = jnp.dot(attn.reshape(ROWS, WIDE), out_weight, preferred_element_type=jnp.float32)
    with jax.named_scope("tp_sum"):
        got = [lax.ppermute(projected, "tp", [(i, i ^ k) for i in range(NTP)]) for k in (1, 2, 3)]
        decode_out = ((projected + got[0]) + (got[1] + got[2])).astype(jnp.bfloat16)

    block_out = block_pass(0, 8, 8, block_lengths, queries, keys, values, one, two, None)
    block_out = block_pass(8, 8, 8, block_lengths, queries, keys, values, one, two, block_out)
    return block_out, decode_out


def solution(mesh):
    return jax.shard_map(
        body,
        mesh=mesh,
        in_specs=(
            P("ctx", "tp"),
            P("ctx", "tp"),
            P("ctx", "tp"),
            P(),
            P("ctx", "tp"),
            P("tp", "ctx"),
        ),
        out_specs=(P("ctx", "tp"), P(None, "ctx")),
        check_vma=False,
    )
```

```python
import functools
import math

import jax
import jax.numpy as jnp
from jax import lax
from jax.experimental import pallas as pl
from jax.experimental.pallas import tpu as pltpu
from jax.sharding import PartitionSpec as P

HEAD = 128
GROUP = 8
KV = 2
SLOTS = 512
HALF = 256
ROWS = 64
NX, NZ, NCORE, NTP = 4, 8, 2, 4
WIDE = KV * GROUP * HEAD
MESSAGE = WIDE + 128
EXP2_SCALE = HEAD**-0.5 * math.log2(math.e)
NEG = -1e30
NT = (((1,), (1,)), ((), ()))


def ctx_at(x, z, core):
    return (x * NZ + z) * NCORE + core


NEAR, FAR = 16, 4
NEAR_GROUPS = [
    [ctx_at(x, 2 * far + z, c) for x in range(NX) for z in range(2) for c in range(NCORE)] for far in range(FAR)
]
FAR_GROUPS = [
    [ctx_at(x, 2 * far + z, c) for far in range(FAR)] for x in range(NX) for z in range(2) for c in range(NCORE)
]
EACH = ROWS // NEAR


def qk(q, k):
    return lax.dot_general(q, k, NT, preferred_element_type=jnp.float32)


def pv(p, v):
    return jnp.dot(p.astype(jnp.bfloat16), v, preferred_element_type=jnp.float32)


def scaled(keys):
    wide = keys.astype(jnp.float32) * EXP2_SCALE
    high = wide.astype(jnp.bfloat16)
    return jnp.concatenate([high, (wide - high.astype(jnp.float32)).astype(jnp.bfloat16)], axis=1)


def with_ones(values):
    return jnp.concatenate([values, jnp.ones_like(values)], axis=1)


def max_of(pieces):
    tiles = [piece[:, i : i + HEAD] for piece in pieces for i in range(0, piece.shape[1], HEAD)]
    return jnp.max(functools.reduce(jnp.maximum, tiles), axis=1, keepdims=True)


def block_kernel(heads, lens, q_ref, k_ref, v_ref, one_ref, two_ref, *rest):
    o_ref = rest[-1]
    ctx = lax.axis_index("ctx")
    own_len, anchor_len = lens[ctx], lens[0]
    row = lax.broadcasted_iota(jnp.int32, (HALF, HALF), 0)
    lane = lax.broadcasted_iota(jnp.int32, (HALF, HALF), 1)

    def run(anchored):
        own_keys, own_values = scaled(k_ref[...]), with_ones(v_ref[...])
        if anchored:
            swap = lax.rem(ctx, NCORE) > 0
            one, two = one_ref[...], two_ref[...]
            anchor_keys = scaled(jnp.where(swap, two, one))
            anchor_values = with_ones(jnp.where(swap, one, two))

        def score(h, part):
            q = q_ref[pl.ds(part * HALF, HALF), h * HEAD : (h + 1) * HEAD]
            q = jnp.concatenate([q, q], axis=1)
            return qk(q, own_keys[: HALF * (part + 1)]), qk(q, anchor_keys) if anchored else None

        def share(part, own, anchor):
            pieces = [own[:, :HALF]] if part else []
            pieces.append(jnp.where(lane <= row, own[:, part * HALF :], NEG))
            if anchored:
                pieces += [anchor[:, :HALF], jnp.where(lane + HALF < anchor_len, anchor[:, HALF:], NEG)]
            top = max_of(pieces)
            shares = [jnp.exp2(piece - top).astype(jnp.bfloat16) for piece in pieces]
            cut = part + 1
            return jnp.concatenate(shares[:cut], axis=1), jnp.concatenate(shares[cut:], axis=1) if anchored else None

        def finish(h, part, own, anchor):
            both = jnp.dot(own, own_values[: HALF * (part + 1)], preferred_element_type=jnp.float32)
            if anchored:
                both += jnp.dot(anchor, anchor_values, preferred_element_type=jnp.float32)
            live = lax.broadcasted_iota(jnp.int32, (HALF, HEAD), 0) + part * HALF < own_len
            out = jnp.where(live, both[:, :HEAD] * (1.0 / both[:, HEAD:]), 0.0)
            o_ref[pl.ds(part * HALF, HALF), h * HEAD : (h + 1) * HEAD] = out.astype(o_ref.dtype)

        items = [(h, part) for h in range(heads) for part in range(2)]
        scores, shares = score(*items[0]), None
        for i, (h, part) in enumerate(items):
            later = score(*items[i + 1]) if i + 1 < len(items) else None
            now = share(part, *scores)
            if shares is not None:
                finish(*items[i - 1], *shares)
            scores, shares = later, now
        finish(*items[-1], *shares)

    pl.when(ctx > 0)(lambda: run(True))
    pl.when(ctx == 0)(lambda: run(False))


def block_pass(first, count, step, lens, queries, keys, values, one, two, out):
    head = lambda g, lens: (0, first // step + g)
    shared = lambda g, lens: (0, (first + g * step) // GROUP)
    specs = [pl.BlockSpec((SLOTS, step * HEAD), head)] + [pl.BlockSpec((SLOTS, HEAD), shared)] * 4
    operands = [queries, keys, values, one, two]
    aliases = {}
    if out is not None:
        specs.append(pl.BlockSpec(memory_space=pl.ANY))
        operands.append(out)
        aliases = {6: 0}
    return pl.pallas_call(
        functools.partial(block_kernel, step),
        grid_spec=pltpu.PrefetchScalarGridSpec(
            num_scalar_prefetch=1,
            grid=(count // step,),
            in_specs=specs,
            out_specs=pl.BlockSpec((SLOTS, step * HEAD), head),
        ),
        out_shape=jax.ShapeDtypeStruct(queries.shape, jnp.bfloat16),
        input_output_aliases=aliases,
        compiler_params=pltpu.CompilerParams(vmem_limit_bytes=56 << 20),
        cost_estimate=pl.CostEstimate(
            flops=count * SLOTS * SLOTS * HEAD * 8, bytes_accessed=4 << 20, transcendentals=count * SLOTS * 1024
        ),
        name="block_pass",
    )(lens, *operands)


def pack_lse(lse):
    lane = lax.broadcasted_iota(jnp.int32, lse.shape, 1)
    high = lse.astype(jnp.bfloat16).astype(jnp.float32)
    rest = lse - high
    mid = rest.astype(jnp.bfloat16).astype(jnp.float32)
    low = rest - mid
    return jnp.where(lane < 16, high, jnp.where(lane < 32, mid, jnp.where(lane < 48, low, 0.0))).astype(jnp.bfloat16)


def spread_kernel(row_ref, o_ref):
    row = row_ref[...].astype(jnp.float32)
    heads = jnp.concatenate([row[:, h * HEAD : (h + 1) * HEAD] for h in range(KV * GROUP)], axis=0)
    o_ref[...] = jnp.broadcast_to(heads.astype(jnp.bfloat16)[None], o_ref.shape)


def spread(row):
    return pl.pallas_call(
        spread_kernel,
        in_specs=[pl.BlockSpec(memory_space=pltpu.VMEM)],
        out_specs=pl.BlockSpec(memory_space=pltpu.VMEM),
        out_shape=jax.ShapeDtypeStruct((ROWS, KV * GROUP, HEAD), jnp.bfloat16),
        compiler_params=pltpu.CompilerParams(vmem_limit_bytes=8 << 20),
        cost_estimate=pl.CostEstimate(flops=1 << 16, bytes_accessed=1 << 18, transcendentals=0),
        name="spread_rows",
    )(row)


def decode_kernel(lens, q_ref, k_ref, v_ref, o_ref):
    own_len = lens[lax.axis_index("ctx")]
    lane = lax.broadcasted_iota(jnp.int32, (ROWS * GROUP, HALF), 1)
    spot = lax.broadcasted_iota(jnp.int32, (ROWS, 128), 1) % 16
    lse = jnp.zeros((ROWS, 128), jnp.float32)

    def put(cols, block):
        for n in range(NEAR):
            o_ref[n, :, cols] = block[n * EACH : (n + 1) * EACH]

    rows = q_ref[...].astype(jnp.float32)
    for kv in range(KV):
        cols = pl.ds(kv * HEAD, HEAD)
        q = rows[:, kv * GROUP : (kv + 1) * GROUP].reshape(ROWS * GROUP, HEAD).astype(jnp.bfloat16)
        scores = qk(q, k_ref[:, cols])
        near, far = scores[:, :HALF], jnp.where(lane + HALF < own_len, scores[:, HALF:], NEG)
        top = jnp.max(jnp.maximum(near, far), axis=1, keepdims=True)
        near, far = jnp.exp2((near - top) * EXP2_SCALE), jnp.exp2((far - top) * EXP2_SCALE)
        total = jnp.sum(near + far, axis=1, keepdims=True)
        weighted = pv(jnp.concatenate([near, far], axis=1), v_ref[:, cols]) * (1.0 / total)
        weighted = weighted.reshape(ROWS, GROUP, HEAD)
        level = jnp.broadcast_to(top * EXP2_SCALE + jnp.log2(total), (ROWS * GROUP, HEAD)).reshape(ROWS, GROUP, HEAD)
        for g in range(GROUP):
            head = kv * GROUP + g
            put(pl.ds(head * HEAD, HEAD), weighted[:, g].astype(jnp.bfloat16))
            lse = jnp.where(spot == head, level[:, g], lse)
    put(pl.ds(WIDE, 128), pack_lse(lse))


def decode(lens, rows, keys, values):
    return pl.pallas_call(
        decode_kernel,
        in_specs=[pl.BlockSpec(memory_space=pltpu.SMEM)] + [pl.BlockSpec(memory_space=pltpu.VMEM)] * 3,
        out_specs=pl.BlockSpec(memory_space=pltpu.VMEM),
        out_shape=jax.ShapeDtypeStruct((NEAR, EACH, MESSAGE), jnp.bfloat16),
        compiler_params=pltpu.CompilerParams(vmem_limit_bytes=32 << 20),
        cost_estimate=pl.CostEstimate(
            flops=4 * KV * GROUP * ROWS * SLOTS * HEAD, bytes_accessed=1 << 20, transcendentals=KV * GROUP * ROWS * SLOTS
        ),
        name="decode_part",
    )(lens, rows, keys, values)


def merge_kernel(last, in_ref, o_ref):
    tiles = in_ref.shape[0] // 2
    tile = lambda t, cols: jnp.concatenate([in_ref[2 * t + i, :, cols].astype(jnp.float32) for i in range(2)], axis=0)

    def across(op, parts):
        half = functools.reduce(op, parts)
        return op(half, pltpu.roll(half, EACH, 0))

    levels = []
    for t in range(tiles):
        parts = tile(t, pl.ds(WIDE, 128))
        levels.append(parts + pltpu.roll(parts, 112, 1) + pltpu.roll(parts, 96, 1))
    top = across(jnp.maximum, levels)
    shares = [jnp.exp2(level - top) for level in levels]
    total = across(jnp.add, shares)
    scale = 1.0 / total
    shares = [share * scale for share in shares]
    for head in range(KV * GROUP):
        cols = pl.ds(head * HEAD, HEAD)
        merged = across(jnp.add, [shares[t][:, head : head + 1] * tile(t, cols) for t in range(tiles)])
        o_ref[:, :, cols] = jnp.broadcast_to(merged[None, :EACH].astype(jnp.bfloat16), (o_ref.shape[0], EACH, HEAD))
    if not last:
        lane = lax.broadcasted_iota(jnp.int32, (2 * EACH, 128), 1)
        level = jnp.where(lane < 16, top + jnp.log2(total), 0.0)
        level = level + pltpu.roll(level, 16, 1) + pltpu.roll(level, 32, 1)
        o_ref[:, :, pl.ds(WIDE, 128)] = jnp.broadcast_to(pack_lse(level)[None, :EACH], (o_ref.shape[0], EACH, 128))


def merge(parts, copies, last):
    return pl.pallas_call(
        functools.partial(merge_kernel, last),
        in_specs=[pl.BlockSpec(memory_space=pltpu.VMEM)],
        out_specs=pl.BlockSpec(memory_space=pltpu.VMEM),
        out_shape=jax.ShapeDtypeStruct((copies, EACH, WIDE if last else MESSAGE), jnp.bfloat16),
        compiler_params=pltpu.CompilerParams(vmem_limit_bytes=8 << 20),
        cost_estimate=pl.CostEstimate(flops=1 << 20, bytes_accessed=1 << 19, transcendentals=1 << 12),
        name="merge_parts",
    )(parts)


def anchor_moves():
    keys_2 = [[((x, 0), (x + dx, dz)) for x in (0, 2)] for dx, dz in ((1, 0), (0, 3), (1, 3))]
    values_2 = [
        [((0, 0), (dx, -dz % NZ)), ((0, 2), (dx, 2 + dz))] for dx, dz in ((0, 2), (2, 0), (2, 2))
    ]
    keys_3 = [
        [((x, 0), (x, near)) for x in range(NX)] + [((x, 3), (x, far)) for x in range(NX)]
        for near, far in ((1, 2), (7, 4), (6, 5))
    ]
    values_3 = [
        [((x, z), (x + dx, z + dz)) for x in (0, 2) for z in (0, 2, 4, 6)] for dx, dz in ((1, 0), (0, 1), (1, 1))
    ]

    def join(keys, values):
        return [
            [(ctx_at(*s, core), ctx_at(*t, core)) for core, pairs in enumerate(both) for s, t in pairs]
            for both in zip(keys, values)
        ]

    return join(keys_2, values_2), join(keys_3, values_3)


def fetch_anchor(keys, values, pins, later_pins):
    ctx = lax.axis_index("ctx")
    perm = lambda block, pairs: lax.ppermute(block, "ctx", pairs)

    def place(held, arrived, moves):
        for block, pairs in zip(arrived, moves):
            hit = functools.reduce(jnp.logical_or, [ctx == target for _, target in pairs])
            held = jnp.where(hit, block, held)
        return held

    with jax.named_scope("anchor_step1"):
        root = ctx_at(0, 0, 0)
        moves = [[(root, ctx_at(2, 0, 0))], [(root, ctx_at(0, 0, 1))], [(root, ctx_at(0, 2, 1))]]
        held = place(keys, [perm(block, pairs) for block, pairs in zip((keys, values, values), moves)], moves)
    for number, moves in enumerate(anchor_moves()):
        with jax.named_scope(f"anchor_step{number + 2}"):
            held, _ = lax.optimization_barrier((held, pins[number]))
            arrived = [perm(held, pairs) for pairs in moves]
            held, _ = lax.optimization_barrier((held, later_pins[number]))
            held = place(held, arrived, moves)
    with jax.named_scope("anchor_swap"):
        other = perm(held, [(i, i ^ 1) for i in range(NX * NZ * NCORE)])
    return held, other


def body(queries, keys, values, block_lengths, decode_query_rows, out_weight):
    with jax.named_scope("rows_out"):
        copies, keys, values = lax.optimization_barrier((spread(decode_query_rows), keys, values))
        rows = lax.all_to_all(copies, "ctx", 0, 0, tiled=True)
    message = decode(block_lengths, rows, keys, values)
    with jax.named_scope("parts_near"):
        parts = lax.all_to_all(message, "ctx", 0, 0, axis_index_groups=NEAR_GROUPS, tiled=True)
    merged = merge(parts, FAR, False)
    one, two = fetch_anchor(keys, values, (keys, message), (keys, keys))
    with jax.named_scope("parts_far"):
        parts = lax.all_to_all(merged, "ctx", 0, 0, axis_index_groups=FAR_GROUPS, tiled=True)
    attn = merge(parts, NEAR, True)
    with jax.named_scope("attn_near"):
        attn = lax.all_to_all(attn, "ctx", 0, 0, axis_index_groups=NEAR_GROUPS, tiled=True)
    projected = jnp.dot(attn.reshape(ROWS, WIDE), out_weight, preferred_element_type=jnp.float32)
    with jax.named_scope("tp_sum"):
        got = [lax.ppermute(projected, "tp", [(i, i ^ k) for i in range(NTP)]) for k in (1, 2, 3)]
        decode_out = ((projected + got[0]) + (got[1] + got[2])).astype(jnp.bfloat16)

    block_out = block_pass(0, 8, 8, block_lengths, queries, keys, values, one, two, None)
    block_out = block_pass(8, 8, 8, block_lengths, queries, keys, values, one, two, block_out)
    return block_out, decode_out


def solution(mesh):
    return jax.shard_map(
        body,
        mesh=mesh,
        in_specs=(
            P("ctx", "tp"),
            P("ctx", "tp"),
            P("ctx", "tp"),
            P(),
            P("ctx", "tp"),
            P("tp", "ctx"),
        ),
        out_specs=(P("ctx", "tp"), P(None, "ctx")),
        check_vma=False,
    )
```

```python
import functools
import math

import jax
import jax.numpy as jnp
from jax import lax
from jax.experimental import pallas as pl
from jax.experimental.pallas import tpu as pltpu
from jax.sharding import PartitionSpec as P

HEAD = 128
GROUP = 8
KV = 2
SLOTS = 512
HALF = 256
ROWS = 64
NX, NZ, NCORE, NTP = 4, 8, 2, 4
WIDE = KV * GROUP * HEAD
MESSAGE = WIDE + 128
EXP2_SCALE = HEAD**-0.5 * math.log2(math.e)
NEG = -1e30
NT = (((1,), (1,)), ((), ()))


def ctx_at(x, z, core):
    return (x * NZ + z) * NCORE + core


NEAR, FAR = 16, 4
NEAR_GROUPS = [
    [ctx_at(x, 2 * far + z, c) for x in range(NX) for z in range(2) for c in range(NCORE)] for far in range(FAR)
]
FAR_GROUPS = [
    [ctx_at(x, 2 * far + z, c) for far in range(FAR)] for x in range(NX) for z in range(2) for c in range(NCORE)
]
EACH = ROWS // NEAR


def qk(q, k):
    return lax.dot_general(q, k, NT, preferred_element_type=jnp.float32)


def pv(p, v):
    return jnp.dot(p.astype(jnp.bfloat16), v, preferred_element_type=jnp.float32)


def scaled(keys):
    wide = keys.astype(jnp.float32) * EXP2_SCALE
    high = wide.astype(jnp.bfloat16)
    return jnp.concatenate([high, (wide - high.astype(jnp.float32)).astype(jnp.bfloat16)], axis=1)


def with_ones(values):
    return jnp.concatenate([values, jnp.ones_like(values)], axis=1)


def max_of(pieces):
    tiles = [piece[:, i : i + HEAD] for piece in pieces for i in range(0, piece.shape[1], HEAD)]
    return jnp.max(functools.reduce(jnp.maximum, tiles), axis=1, keepdims=True)


def block_kernel(heads, lens, q_ref, k_ref, v_ref, one_ref, two_ref, *rest):
    o_ref = rest[-1]
    ctx = lax.axis_index("ctx")
    own_len, anchor_len = lens[ctx], lens[0]
    row = lax.broadcasted_iota(jnp.int32, (HALF, HALF), 0)
    lane = lax.broadcasted_iota(jnp.int32, (HALF, HALF), 1)

    def run(anchored):
        own_keys, own_values = scaled(k_ref[...]), with_ones(v_ref[...])
        if anchored:
            swap = lax.rem(ctx, NCORE) > 0
            one, two = one_ref[...], two_ref[...]
            anchor_keys = scaled(jnp.where(swap, two, one))
            anchor_values = with_ones(jnp.where(swap, one, two))

        def score(h, part):
            q = q_ref[pl.ds(part * HALF, HALF), h * HEAD : (h + 1) * HEAD]
            q = jnp.concatenate([q, q], axis=1)
            return qk(q, own_keys[: HALF * (part + 1)]), qk(q, anchor_keys) if anchored else None

        def share(part, own, anchor):
            pieces = [own[:, :HALF]] if part else []
            pieces.append(jnp.where(lane <= row, own[:, part * HALF :], NEG))
            if anchored:
                pieces += [anchor[:, :HALF], jnp.where(lane + HALF < anchor_len, anchor[:, HALF:], NEG)]
            top = max_of(pieces)
            shares = [jnp.exp2(piece - top).astype(jnp.bfloat16) for piece in pieces]
            cut = part + 1
            return jnp.concatenate(shares[:cut], axis=1), jnp.concatenate(shares[cut:], axis=1) if anchored else None

        def finish(h, part, own, anchor):
            both = jnp.dot(own, own_values[: HALF * (part + 1)], preferred_element_type=jnp.float32)
            if anchored:
                both += jnp.dot(anchor, anchor_values, preferred_element_type=jnp.float32)
            live = lax.broadcasted_iota(jnp.int32, (HALF, HEAD), 0) + part * HALF < own_len
            out = jnp.where(live, both[:, :HEAD] * (1.0 / both[:, HEAD:]), 0.0)
            o_ref[pl.ds(part * HALF, HALF), h * HEAD : (h + 1) * HEAD] = out.astype(o_ref.dtype)

        items = [(h, part) for h in range(heads) for part in range(2)]
        scores, shares = score(*items[0]), None
        for i, (h, part) in enumerate(items):
            later = score(*items[i + 1]) if i + 1 < len(items) else None
            now = share(part, *scores)
            if shares is not None:
                finish(*items[i - 1], *shares)
            scores, shares = later, now
        finish(*items[-1], *shares)

    pl.when(ctx > 0)(lambda: run(True))
    pl.when(ctx == 0)(lambda: run(False))


def block_pass(first, count, step, lens, queries, keys, values, one, two, out):
    head = lambda g, lens: (0, first // step + g)
    shared = lambda g, lens: (0, (first + g * step) // GROUP)
    specs = [pl.BlockSpec((SLOTS, step * HEAD), head)] + [pl.BlockSpec((SLOTS, HEAD), shared)] * 4
    operands = [queries, keys, values, one, two]
    aliases = {}
    if out is not None:
        specs.append(pl.BlockSpec(memory_space=pl.ANY))
        operands.append(out)
        aliases = {6: 0}
    return pl.pallas_call(
        functools.partial(block_kernel, step),
        grid_spec=pltpu.PrefetchScalarGridSpec(
            num_scalar_prefetch=1,
            grid=(count // step,),
            in_specs=specs,
            out_specs=pl.BlockSpec((SLOTS, step * HEAD), head),
        ),
        out_shape=jax.ShapeDtypeStruct(queries.shape, jnp.bfloat16),
        input_output_aliases=aliases,
        compiler_params=pltpu.CompilerParams(vmem_limit_bytes=56 << 20),
        cost_estimate=pl.CostEstimate(
            flops=count * SLOTS * SLOTS * HEAD * 8, bytes_accessed=4 << 20, transcendentals=count * SLOTS * 1024
        ),
        name="block_pass",
    )(lens, *operands)


def pack_lse(lse):
    lane = lax.broadcasted_iota(jnp.int32, lse.shape, 1)
    high = lse.astype(jnp.bfloat16).astype(jnp.float32)
    rest = lse - high
    mid = rest.astype(jnp.bfloat16).astype(jnp.float32)
    low = rest - mid
    return jnp.where(lane < 16, high, jnp.where(lane < 32, mid, jnp.where(lane < 48, low, 0.0))).astype(jnp.bfloat16)


def spread_kernel(row_ref, o_ref):
    row = row_ref[...].astype(jnp.float32)
    heads = jnp.concatenate([row[:, h * HEAD : (h + 1) * HEAD] for h in range(KV * GROUP)], axis=0)
    o_ref[...] = jnp.broadcast_to(heads.astype(jnp.bfloat16)[None], o_ref.shape)


def spread(row):
    return pl.pallas_call(
        spread_kernel,
        in_specs=[pl.BlockSpec(memory_space=pltpu.VMEM)],
        out_specs=pl.BlockSpec(memory_space=pltpu.VMEM),
        out_shape=jax.ShapeDtypeStruct((ROWS, KV * GROUP, HEAD), jnp.bfloat16),
        compiler_params=pltpu.CompilerParams(vmem_limit_bytes=8 << 20),
        cost_estimate=pl.CostEstimate(flops=1 << 16, bytes_accessed=1 << 18, transcendentals=0),
        name="spread_rows",
    )(row)


def decode_kernel(lens, q_ref, k_ref, v_ref, o_ref):
    own_len = lens[lax.axis_index("ctx")]
    lane = lax.broadcasted_iota(jnp.int32, (ROWS * GROUP, HALF), 1)
    spot = lax.broadcasted_iota(jnp.int32, (ROWS, 128), 1) % 16
    lse = jnp.zeros((ROWS, 128), jnp.float32)

    def put(cols, block):
        for n in range(NEAR):
            o_ref[n, :, cols] = block[n * EACH : (n + 1) * EACH]

    rows = q_ref[...].astype(jnp.float32)
    for kv in range(KV):
        cols = pl.ds(kv * HEAD, HEAD)
        q = rows[:, kv * GROUP : (kv + 1) * GROUP].reshape(ROWS * GROUP, HEAD).astype(jnp.bfloat16)
        scores = qk(q, k_ref[:, cols])
        near, far = scores[:, :HALF], jnp.where(lane + HALF < own_len, scores[:, HALF:], NEG)
        top = jnp.max(jnp.maximum(near, far), axis=1, keepdims=True)
        near, far = jnp.exp2((near - top) * EXP2_SCALE), jnp.exp2((far - top) * EXP2_SCALE)
        total = jnp.sum(near + far, axis=1, keepdims=True)
        weighted = pv(jnp.concatenate([near, far], axis=1), v_ref[:, cols]) * (1.0 / total)
        weighted = weighted.reshape(ROWS, GROUP, HEAD)
        level = jnp.broadcast_to(top * EXP2_SCALE + jnp.log2(total), (ROWS * GROUP, HEAD)).reshape(ROWS, GROUP, HEAD)
        for g in range(GROUP):
            head = kv * GROUP + g
            put(pl.ds(head * HEAD, HEAD), weighted[:, g].astype(jnp.bfloat16))
            lse = jnp.where(spot == head, level[:, g], lse)
    put(pl.ds(WIDE, 128), pack_lse(lse))


def decode(lens, rows, keys, values):
    return pl.pallas_call(
        decode_kernel,
        in_specs=[pl.BlockSpec(memory_space=pltpu.SMEM)] + [pl.BlockSpec(memory_space=pltpu.VMEM)] * 3,
        out_specs=pl.BlockSpec(memory_space=pltpu.VMEM),
        out_shape=jax.ShapeDtypeStruct((NEAR, EACH, MESSAGE), jnp.bfloat16),
        compiler_params=pltpu.CompilerParams(vmem_limit_bytes=32 << 20),
        cost_estimate=pl.CostEstimate(
            flops=4 * KV * GROUP * ROWS * SLOTS * HEAD, bytes_accessed=1 << 20, transcendentals=KV * GROUP * ROWS * SLOTS
        ),
        name="decode_part",
    )(lens, rows, keys, values)


def merge_kernel(last, in_ref, o_ref):
    tiles = in_ref.shape[0] // 2
    tile = lambda t, cols: jnp.concatenate([in_ref[2 * t + i, :, cols].astype(jnp.float32) for i in range(2)], axis=0)

    def across(op, parts):
        half = functools.reduce(op, parts)
        return op(half, pltpu.roll(half, EACH, 0))

    levels = []
    for t in range(tiles):
        parts = tile(t, pl.ds(WIDE, 128))
        levels.append(parts + pltpu.roll(parts, 112, 1) + pltpu.roll(parts, 96, 1))
    top = across(jnp.maximum, levels)
    shares = [jnp.exp2(level - top) for level in levels]
    total = across(jnp.add, shares)
    scale = 1.0 / total
    shares = [share * scale for share in shares]
    for head in range(KV * GROUP):
        cols = pl.ds(head * HEAD, HEAD)
        merged = across(jnp.add, [shares[t][:, head : head + 1] * tile(t, cols) for t in range(tiles)])
        o_ref[:, :, cols] = jnp.broadcast_to(merged[None, :EACH].astype(jnp.bfloat16), (o_ref.shape[0], EACH, HEAD))
    if not last:
        lane = lax.broadcasted_iota(jnp.int32, (2 * EACH, 128), 1)
        level = jnp.where(lane < 16, top + jnp.log2(total), 0.0)
        level = level + pltpu.roll(level, 16, 1) + pltpu.roll(level, 32, 1)
        o_ref[:, :, pl.ds(WIDE, 128)] = jnp.broadcast_to(pack_lse(level)[None, :EACH], (o_ref.shape[0], EACH, 128))


def merge(parts, copies, last):
    return pl.pallas_call(
        functools.partial(merge_kernel, last),
        in_specs=[pl.BlockSpec(memory_space=pltpu.VMEM)],
        out_specs=pl.BlockSpec(memory_space=pltpu.VMEM),
        out_shape=jax.ShapeDtypeStruct((copies, EACH, WIDE if last else MESSAGE), jnp.bfloat16),
        compiler_params=pltpu.CompilerParams(vmem_limit_bytes=8 << 20),
        cost_estimate=pl.CostEstimate(flops=1 << 20, bytes_accessed=1 << 19, transcendentals=1 << 12),
        name="merge_parts",
    )(parts)


def anchor_moves():
    keys_2 = [
        [((0, 0), (dx, dz)), ((3, 0), (3 - dx, dz))] for dx, dz in ((1, 0), (0, 3), (1, 3))
    ]
    values_2 = [
        [((0, 0), (dx, 6 * dz)), ((0, 1), (dx, 1 + 2 * dz))] for dx, dz in ((0, 1), (2, 0), (2, 1))
    ]
    keys_3 = [
        [((x, 0), (x, near)) for x in range(NX)] + [((x, 3), (x, far)) for x in range(NX)]
        for near, far in ((1, 2), (7, 4), (6, 5))
    ]
    values_3 = [
        [((x, z), (x + dx, beside if dz else z)) for x in (0, 2) for z, beside in ((0, 7), (1, 2), (3, 4), (6, 5))]
        for dx, dz in ((1, 0), (0, 1), (1, 1))
    ]

    def join(keys, values):
        return [
            [(ctx_at(*s, core), ctx_at(*t, core)) for core, pairs in enumerate(both) for s, t in pairs]
            for both in zip(keys, values)
        ]

    return join(keys_2, values_2), join(keys_3, values_3)


def fetch_anchor(keys, values, pins, later_pins):
    ctx = lax.axis_index("ctx")
    perm = lambda block, pairs: lax.ppermute(block, "ctx", pairs)

    def place(held, arrived, moves):
        for block, pairs in zip(arrived, moves):
            hit = functools.reduce(jnp.logical_or, [ctx == target for _, target in pairs])
            held = jnp.where(hit, block, held)
        return held

    with jax.named_scope("anchor_step1"):
        root = ctx_at(0, 0, 0)
        moves = [[(root, ctx_at(3, 0, 0))], [(root, ctx_at(0, 0, 1))], [(root, ctx_at(0, 1, 1))]]
        held = place(keys, [perm(block, pairs) for block, pairs in zip((keys, values, values), moves)], moves)
    for number, moves in enumerate(anchor_moves()):
        with jax.named_scope(f"anchor_step{number + 2}"):
            held, _ = lax.optimization_barrier((held, pins[number]))
            arrived = [perm(held, pairs) for pairs in moves]
            held, _ = lax.optimization_barrier((held, later_pins[number]))
            held = place(held, arrived, moves)
    with jax.named_scope("anchor_swap"):
        other = perm(held, [(i, i ^ 1) for i in range(NX * NZ * NCORE)])
    return held, other


def body(queries, keys, values, block_lengths, decode_query_rows, out_weight):
    with jax.named_scope("rows_out"):
        copies, keys, values = lax.optimization_barrier((spread(decode_query_rows), keys, values))
        rows = lax.all_to_all(copies, "ctx", 0, 0, tiled=True)
    message = decode(block_lengths, rows, keys, values)
    with jax.named_scope("parts_near"):
        parts = lax.all_to_all(message, "ctx", 0, 0, axis_index_groups=NEAR_GROUPS, tiled=True)
    merged = merge(parts, FAR, False)
    one, two = fetch_anchor(keys, values, (keys, message), (keys, keys))
    with jax.named_scope("parts_far"):
        parts = lax.all_to_all(merged, "ctx", 0, 0, axis_index_groups=FAR_GROUPS, tiled=True)
    attn = merge(parts, NEAR, True)
    with jax.named_scope("attn_near"):
        attn = lax.all_to_all(attn, "ctx", 0, 0, axis_index_groups=NEAR_GROUPS, tiled=True)
    projected = jnp.dot(attn.reshape(ROWS, WIDE), out_weight, preferred_element_type=jnp.float32)
    with jax.named_scope("tp_sum"):
        got = [lax.ppermute(projected, "tp", [(i, i ^ k) for i in range(NTP)]) for k in (1, 2, 3)]
        decode_out = ((projected + got[0]) + (got[1] + got[2])).astype(jnp.bfloat16)

    block_out = block_pass(0, 8, 8, block_lengths, queries, keys, values, one, two, None)
    block_out = block_pass(8, 8, 8, block_lengths, queries, keys, values, one, two, block_out)
    return block_out, decode_out


def solution(mesh):
    return jax.shard_map(
        body,
        mesh=mesh,
        in_specs=(
            P("ctx", "tp"),
            P("ctx", "tp"),
            P("ctx", "tp"),
            P(),
            P("ctx", "tp"),
            P("tp", "ctx"),
        ),
        out_specs=(P("ctx", "tp"), P(None, "ctx")),
        check_vma=False,
    )
```
